512 devices in a mesh: replica: 16 (over x_hi, y, core), tensor: 32 (over z, x_lo).
Axes of the slice: x: 4 (x_hi: 2, x_lo: 2; x = x_hi * 2 + x_lo), y: 4, z: 16, core: 2. Of those that a mesh axis runs over, the one named last changes fastest.
Arguments:
- step: int32 [1], replicated, may hold values from 0 to 999
- head_outputs: bfloat16 [16, 1536, 4096], P('replica', None, 'tensor'), may hold values from -70 to 70
- out_weight: bfloat16 [16, 4096, 5120], P('replica', 'tensor'), may hold values from -6 to 6
- cotangent: bfloat16 [16, 1536, 5120], P('replica', 'tensor'), may hold values from -40 to 40
Outputs:
- new_weight: bfloat16 [16, 4096, 5120], P('replica', 'tensor')
- head_grads: bfloat16 [16, 1536, 4096], P('replica', None, 'tensor')
The draws below stay inside these ranges and needn't reach their ends.
All inputs are finite; a program needn't handle non-finite values.
Results may differ from the reference program's by a relative error of at most 0.0052.
Values may be sent and summed in bfloat16 or wider, within the bound.
No kernel may reach another device: no remote copies, remote signals or barrier semaphores. Data moves between devices by JAX's collectives and lax.ppermute only.
A program may use at most 64 MiB of HBM per device.

```python
import math
import jax
import jax.numpy as jnp
from jax import lax

D = 5120
HD = 128
HEADS = 32
FEATS = 4096
TOKENS = 1536
REPLICAS = 16
LEVELS = 3


def column_scales(key, count, rise):
    spread = jnp.exp(jax.random.uniform(key, (count,), jnp.float32) * math.log(10.0))
    heads_of = (jnp.arange(count) // HD).astype(jnp.float32)
    return spread * jnp.power(3.0, rise * heads_of / max(HEADS - 1, 1))


def base_values(key, shape):
    first = jax.random.fold_in(key, 0)
    return jnp.clip(jax.random.normal(first, shape, jnp.float32), -4.0, 4.0)


def draw_head_outputs(key, part):
    key = jax.random.fold_in(key, 11)
    scale_key, value_key = jax.random.split(key)
    values = base_values(value_key, (REPLICAS, TOKENS, FEATS))
    return (values * column_scales(scale_key, FEATS, 0.5)).astype(jnp.bfloat16)


def draw_cotangent(key, part):
    key = jax.random.fold_in(key, 23)
    scale_key, value_key = jax.random.split(key)
    values = base_values(value_key, (REPLICAS, TOKENS, D))
    return (values * column_scales(scale_key, D, 0.0)).astype(jnp.bfloat16)


def shard_levels(stream_key, dims, pieces, low, largest):
    def one(dim, parts):
        heights = jax.random.uniform(jax.random.fold_in(jax.random.fold_in(stream_key, 6), dim), (parts,), jnp.float32, low / len(pieces), largest / len(pieces))
        return jnp.repeat(jnp.exp(heights), dims[dim] // parts).reshape((-1,) + (1,) * (len(dims) - dim - 1))

    factor_of = one(*pieces[0])
    for cut in pieces[1:]:
        factor_of = factor_of * one(*cut)
    return factor_of


def centred(rng, extent, scale, limit, cuts=(), kind=jnp.bfloat16):
    values = scale * jax.random.normal(rng, extent, jnp.float32)
    if cuts:
        values = values * shard_levels(rng, extent, cuts, -0.22, 0.18)
    return jnp.clip(values, -limit, limit).astype(kind)


def setup_inputs(seed: int = 0) -> dict:
    key_of = jax.random.split(jax.random.key(seed), 5)
    return {
        "step": jax.random.randint(key_of[0], (1,), 0, 1000).astype(jnp.int32),
        "head_outputs": draw_head_outputs(jax.random.fold_in(key_of[4], 71), 0),
        "out_weight": centred(key_of[2], (REPLICAS, FEATS, D), 1.0, 6.0, ((0, 16), (1, 32))),
        "cotangent": draw_cotangent(jax.random.fold_in(key_of[4], 71), 0),
    }


step_rate = 0.5

def one_group(head_outputs, out_weight, cotangent):
    multiplier = float(FEATS) ** (-0.5)
    gradient = multiplier * lax.dot_general(head_outputs, cotangent, (((0,), (0,)), ((), ())), preferred_element_type=jnp.float32)
    head_grads = (multiplier * lax.dot_general(cotangent, out_weight, (((1,), (1,)), ((), ())), preferred_element_type=jnp.float32)).astype(jnp.bfloat16)
    squares = jnp.sum(gradient * gradient)
    factor = jnp.minimum(1.0, jnp.sqrt(jnp.float32(FEATS * D)) / jnp.sqrt(squares))
    stepped = (out_weight.astype(jnp.float32) - step_rate * factor * gradient).astype(jnp.bfloat16)
    return (stepped, head_grads)

def reference(step, head_outputs, out_weight, cotangent):
    stepped, head_grads = lax.map(lambda items: one_group(items[0], items[1], items[2]), (head_outputs, out_weight, cotangent))
    bit_index = step[0] % LEVELS
    distance = jnp.where(bit_index == 0, 1, jnp.where(bit_index == 1, 2, 4)).astype(jnp.int32)
    groups = jnp.arange(REPLICAS, dtype=jnp.int32)
    partner = jnp.where(groups // distance % 2 == 0, groups + distance, groups - distance).astype(jnp.int32)
    others = jnp.take(stepped, partner, axis=0)
    new_weight = ((stepped.astype(jnp.float32) + others.astype(jnp.float32)) * 0.5).astype(jnp.bfloat16)
    return (new_weight, head_grads)
```

```python
from functools import partial

import jax
import jax.numpy as jnp
from jax import lax
from jax.sharding import Mesh, PartitionSpec as P

step_rate = 0.5
LEVELS = 3
PAIR = [(0, 1), (1, 0)]
Z = ("zh", "zl")


def to_partner(block, level):
    if level == 0:
        return lax.ppermute(block, "core", PAIR)
    return lax.ppermute(block, "y", [(i, i ^ level) for i in range(4)])


def one_step(level, head_outputs, out_weight, cotangent):
    heads = head_outputs[0]
    weight = out_weight[0]
    tokens = cotangent[0]
    rows, width = weight.shape
    half = width // 2
    features = rows * 32
    multiplier = float(features) ** (-0.5)
    x = lax.axis_index("x")

    def mine(block):
        return lax.dynamic_slice_in_dim(block, x * half, half, axis=1)

    def other(block):
        return lax.dynamic_slice_in_dim(block, (1 - x) * half, half, axis=1)

    def swap(block):
        return lax.ppermute(block, "x", PAIR)

    kept = mine(tokens)
    got = swap(other(tokens))
    pair_tokens = jnp.where(
        x == 0, jnp.concatenate([kept, got], 0), jnp.concatenate([got, kept], 0)
    )
    gathered = lax.all_gather(pair_tokens, Z, axis=0, tiled=True)

    heads_pair = jnp.concatenate([heads, swap(heads)], 1)
    weight_pair = jnp.concatenate([mine(weight), swap(other(weight))], 0)
    partner_weight = to_partner(weight, level)

    grad = multiplier * lax.dot_general(
        heads_pair, gathered, (((0,), (0,)), ((), ())), preferred_element_type=jnp.float32
    )
    squares = jnp.sum(grad * grad)
    grad16 = grad.astype(jnp.bfloat16)
    grad_here = grad16[:rows]
    grad_there = swap(grad16[rows:])
    partner_here = to_partner(grad_here, level)
    partner_there = to_partner(grad_there, level)

    squares = lax.psum(squares, "zl")
    squares = lax.psum(squares, "zh")
    squares = lax.psum(squares, "x")
    partner_squares = to_partner(squares, level)

    partial_heads = lax.dot_general(
        gathered, weight_pair, (((1,), (1,)), ((), ())), preferred_element_type=jnp.float32
    )
    from_pair = swap(partial_heads[:, rows:].astype(jnp.bfloat16))
    head_grads = (
        multiplier * (partial_heads[:, :rows] + from_pair.astype(jnp.float32))
    ).astype(jnp.bfloat16)

    def factor_of(total):
        return jnp.minimum(1.0, jnp.sqrt(jnp.float32(features * width)) / jnp.sqrt(total))

    def stepped(block, factor, gradient):
        new = block.astype(jnp.float32) - step_rate * factor * gradient.astype(jnp.float32)
        return new.astype(jnp.bfloat16).astype(jnp.float32)

    factor, partner_factor = factor_of(squares), factor_of(partner_squares)

    def both(here, there):
        return jnp.where(
            x == 0, jnp.concatenate([here, there], 1), jnp.concatenate([there, here], 1)
        )

    new_weight = (
        (
            stepped(weight, factor, both(grad_here, grad_there))
            + stepped(partner_weight, partner_factor, both(partner_here, partner_there))
        )
        * 0.5
    ).astype(jnp.bfloat16)
    return (new_weight[None], head_grads[None])


def per_device(step, head_outputs, out_weight, cotangent):
    branches = [partial(one_step, level) for level in range(LEVELS)]
    return lax.switch(step[0] % LEVELS, branches, head_outputs, out_weight, cotangent)


def solution(mesh):
    mesh = Mesh(
        mesh.devices.reshape(2, 4, 2, 4, 4, 2), ("x_hi", "y", "core", "zh", "zl", "x")
    )
    replica = ("x_hi", "y", "core")
    tensor = ("zh", "zl", "x")
    return jax.shard_map(
        per_device,
        mesh=mesh,
        in_specs=(
            P(),
            P(replica, None, tensor),
            P(replica, tensor, None),
            P(replica, tensor, None),
        ),
        out_specs=(P(replica, tensor, None), P(replica, None, tensor)),
        check_vma=False,
    )
```

```python
from functools import partial

import jax
import jax.numpy as jnp
from jax import lax
from jax.experimental import pallas as pl
from jax.experimental.pallas import tpu as pltpu
from jax.sharding import Mesh, PartitionSpec as P

step_rate = 0.5
PAIR = [(0, 1), (1, 0)]
Z = ("zh", "zl")
PARTNER_AXES = ("core", "yl", "yh")
VMEM_BYTES = 48 * 1024 * 1024


def products_kernel(
    heads_ref, tokens_ref, weight_ref, here_ref, there_ref, squares_ref, part_here_ref,
    part_there_ref, total, sums,
):
    rows = here_ref.shape[0]
    step, last = pl.program_id(0), pl.num_programs(0) - 1
    block = tokens_ref[...]
    grad = jnp.dot(heads_ref[...], block, preferred_element_type=jnp.float32)
    here_ref[...] = grad[:rows].astype(here_ref.dtype)
    there_ref[...] = grad[rows:].astype(there_ref.dtype)
    part = lax.dot_general(
        block, weight_ref[...], (((1,), (1,)), ((), ())), preferred_element_type=jnp.float32
    )
    column_sums = jnp.sum(grad * grad, axis=0, keepdims=True)

    @pl.when(step == 0)
    def _():
        total[...] = part
        sums[...] = column_sums

    @pl.when(step > 0)
    def _():
        total[...] += part
        sums[...] += column_sums

    @pl.when(step == last)
    def _():
        part_here_ref[...] = total[:, :rows]
        part_there_ref[...] = total[:, rows:].astype(part_there_ref.dtype)
        squares_ref[0, 0] = jnp.sum(sums[...])


def products(heads_t, tokens, weight, blocks=5):
    pair_rows, count = heads_t.shape
    rows, width = pair_rows // 2, tokens.shape[1]
    cols = width // blocks
    return pl.pallas_call(
        products_kernel,
        grid=(blocks,),
        in_specs=[
            pl.BlockSpec((pair_rows, count), lambda i: (0, 0)),
            pl.BlockSpec((count, cols), lambda i: (0, i)),
            pl.BlockSpec((pair_rows, cols), lambda i: (0, i)),
        ],
        out_specs=[
            pl.BlockSpec((rows, cols), lambda i: (0, i)),
            pl.BlockSpec((rows, cols), lambda i: (0, i)),
            pl.BlockSpec((1, 1), lambda i: (0, 0), memory_space=pltpu.SMEM),
            pl.BlockSpec((count, rows), lambda i: (0, 0)),
            pl.BlockSpec((count, rows), lambda i: (0, 0)),
        ],
        out_shape=[
            jax.ShapeDtypeStruct((rows, width), jnp.bfloat16),
            jax.ShapeDtypeStruct((rows, width), jnp.bfloat16),
            jax.ShapeDtypeStruct((1, 1), jnp.float32),
            jax.ShapeDtypeStruct((count, rows), jnp.float32),
            jax.ShapeDtypeStruct((count, rows), jnp.bfloat16),
        ],
        scratch_shapes=[
            pltpu.VMEM((count, pair_rows), jnp.float32),
            pltpu.VMEM((1, cols), jnp.float32),
        ],
        compiler_params=pltpu.CompilerParams(vmem_limit_bytes=VMEM_BYTES),
        cost_estimate=pl.CostEstimate(
            flops=4 * pair_rows * count * width,
            bytes_accessed=2 * (count * width + 3 * pair_rows * width + 4 * count * rows),
            transcendentals=0,
        ),
        name="products",
    )(heads_t, tokens, weight)


def finish_kernel(
    multiplier, spot_ref, squares_ref, weight_ref, partner_ref, here_ref, there_ref,
    partner_here_ref, partner_there_ref, part_ref, from_pair_ref, new_ref, heads_ref,
):
    entries = jnp.float32(4096 * 5120)
    here = pl.program_id(0) == 0
    own = spot_ref[1]

    def scale(index):
        total = jnp.full((8, 128), squares_ref[index], jnp.float32) * (multiplier * multiplier)
        factor = jnp.minimum(1.0, jnp.sqrt(entries) / jnp.sqrt(total))
        return (step_rate * multiplier * factor)[:1, :1]

    def stepped(block_ref, amount, first_ref, second_ref):
        grad = jnp.where(here, first_ref[...], second_ref[...]).astype(jnp.float32)
        new = block_ref[...].astype(jnp.float32) - amount * grad
        return new.astype(jnp.bfloat16).astype(jnp.float32)

    mine = stepped(weight_ref, scale(own), here_ref, there_ref)
    theirs = stepped(partner_ref, scale(1 - own), partner_here_ref, partner_there_ref)
    new_ref[...] = ((mine + theirs) * 0.5).astype(new_ref.dtype)
    heads_ref[...] = (
        multiplier * (part_ref[...] + from_pair_ref[...].astype(jnp.float32))
    ).astype(heads_ref.dtype)


def finish(multiplier, spot, squares, weight, partner, grads, partner_grads, part, from_pair, blocks=2):
    rows, width = weight.shape
    half = width // 2
    cols = half // blocks
    count = part.shape[0]
    piece = count // (2 * blocks)

    def whole(h, i, spot_ref, squares_ref):
        return (0, jnp.where(h == 0, spot_ref[0], 1 - spot_ref[0]) * blocks + i)

    first = lambda h, i, *_: (0, jnp.where(h == 0, i, blocks - 1))
    second = lambda h, i, *_: (0, jnp.where(h == 0, 0, i))
    down = lambda h, i, *_: (h * blocks + i, 0)
    wide = pl.BlockSpec((rows, cols), whole)
    return pl.pallas_call(
        partial(finish_kernel, multiplier),
        grid_spec=pltpu.PrefetchScalarGridSpec(
            num_scalar_prefetch=2,
            grid=(2, blocks),
            in_specs=[
                wide,
                wide,
                pl.BlockSpec((rows, cols), first),
                pl.BlockSpec((rows, cols), second),
                pl.BlockSpec((rows, cols), first),
                pl.BlockSpec((rows, cols), second),
                pl.BlockSpec((piece, rows), down),
                pl.BlockSpec((piece, rows), down),
            ],
            out_specs=[wide, pl.BlockSpec((piece, rows), down)],
        ),
        out_shape=[
            jax.ShapeDtypeStruct((rows, width), jnp.bfloat16),
            jax.ShapeDtypeStruct((count, rows), jnp.bfloat16),
        ],
        compiler_params=pltpu.CompilerParams(vmem_limit_bytes=VMEM_BYTES),
        cost_estimate=pl.CostEstimate(
            flops=8 * rows * width, bytes_accessed=10 * rows * width + 8 * count * rows,
            transcendentals=0,
        ),
        name="finish",
    )(spot, squares, weight, partner, *grads, *partner_grads, part, from_pair)


def one_step(level, head_outputs, out_weight, cotangent):
    heads = head_outputs[0]
    weight = out_weight[0]
    tokens = cotangent[0]
    rows, width = weight.shape
    half = width // 2
    partner_axis = PARTNER_AXES[level]
    x = lax.axis_index("x")
    own = lax.axis_index(partner_axis)

    def mine(block):
        return lax.dynamic_slice_in_dim(block, x * half, half, axis=1)

    def other(block):
        return lax.dynamic_slice_in_dim(block, (1 - x) * half, half, axis=1)

    def swap(block):
        return lax.ppermute(block, "x", PAIR)

    def to_partner(block):
        return lax.ppermute(block, partner_axis, PAIR)

    kept = mine(tokens)
    got = swap(other(tokens))
    pair_tokens = jnp.where(
        x == 0, jnp.concatenate([kept, got], 0), jnp.concatenate([got, kept], 0)
    )
    gathered = lax.all_gather(pair_tokens, Z, axis=0, tiled=True)

    heads_t = jnp.concatenate([heads, swap(heads)], 1).T
    weight_pair = jnp.concatenate([mine(weight), swap(other(weight))], 0)
    partner_weight = to_partner(weight)

    gathered, partner_weight = lax.optimization_barrier((gathered, partner_weight))
    here, there, squares, part_here, part_there = products(heads_t, gathered, weight_pair)
    there = swap(there)
    partner_here = to_partner(here)
    squares = jnp.where(jnp.arange(2) == own, squares[0, 0], 0.0)
    squares = lax.psum(squares, "zl")
    squares, there = lax.optimization_barrier((squares, there))
    partner_there = to_partner(there)
    squares = lax.psum(squares, "zh")
    squares, part_there = lax.optimization_barrier((squares, part_there))
    from_pair = swap(part_there)
    squares = lax.psum(squares, (partner_axis, "x"))

    return (
        own, squares, partner_weight, (here, there), (partner_here, partner_there), part_here,
        from_pair,
    )


def per_device(step, head_outputs, out_weight, cotangent):
    branches = [partial(one_step, level) for level in range(len(PARTNER_AXES))]
    own, squares, partner_weight, grads, partner_grads, part_here, from_pair = lax.switch(
        step[0] % len(PARTNER_AXES), branches, head_outputs, out_weight, cotangent
    )
    weight = out_weight[0]
    new_weight, head_grads = finish(
        float(weight.shape[0] * 32) ** (-0.5),
        jnp.stack([lax.axis_index("x"), own]).astype(jnp.int32),
        squares,
        weight,
        partner_weight,
        grads,
        partner_grads,
        part_here,
        from_pair,
    )
    return (new_weight[None], head_grads[None])


def solution(mesh):
    mesh = Mesh(
        mesh.devices.reshape(2, 2, 2, 2, 4, 4, 2), ("x_hi", "yh", "yl", "core", "zh", "zl", "x")
    )
    replica = ("x_hi", "yh", "yl", "core")
    tensor = ("zh", "zl", "x")
    return jax.shard_map(
        per_device,
        mesh=mesh,
        in_specs=(
            P(),
            P(replica, None, tensor),
            P(replica, tensor, None),
            P(replica, tensor, None),
        ),
        out_specs=(P(replica, tensor, None), P(replica, None, tensor)),
        check_vma=False,
    )
```

```python
from functools import partial

import jax
import jax.numpy as jnp
from jax import lax
from jax.experimental import pallas as pl
from jax.experimental.pallas import tpu as pltpu
from jax.sharding import Mesh, PartitionSpec as P

step_rate = 0.5
PAIR = [(0, 1), (1, 0)]
Z = ("zh", "zl")
PARTNER_AXES = ("core", "yl", "yh")
VMEM_BYTES = 48 * 1024 * 1024
SUMMED = 64


def products_kernel(
    heads_ref, tokens_ref, weight_ref, here_ref, there_ref, squares_ref, part_here_ref,
    part_there_ref, total, sums,
):
    rows = here_ref.shape[0]
    step, last = pl.program_id(0), pl.num_programs(0) - 1
    block = tokens_ref[...]
    grad = jnp.dot(heads_ref[...], block, preferred_element_type=jnp.float32)
    here_ref[...] = grad[:rows].astype(here_ref.dtype)
    there_ref[...] = grad[rows:].astype(there_ref.dtype)
    part = lax.dot_general(
        block, weight_ref[...], (((1,), (1,)), ((), ())), preferred_element_type=jnp.float32
    )
    column_sums = jnp.sum(grad * grad, axis=0, keepdims=True)

    @pl.when(step == 0)
    def _():
        total[...] = part
        sums[...] = column_sums

    @pl.when(step > 0)
    def _():
        total[...] += part
        sums[...] += column_sums

    @pl.when(step == last)
    def _():
        part_here_ref[...] = total[:, :rows]
        part_there_ref[...] = total[:, rows:].astype(part_there_ref.dtype)
        squares_ref[...] = jnp.full(squares_ref.shape, jnp.sum(sums[...]), jnp.float32)


def products(heads_t, tokens, weight, blocks=4):
    pair_rows, count = heads_t.shape
    rows, width = pair_rows // 2, tokens.shape[1]
    cols = width // blocks
    return pl.pallas_call(
        products_kernel,
        grid=(blocks,),
        in_specs=[
            pl.BlockSpec((pair_rows, count), lambda i: (0, 0)),
            pl.BlockSpec((count, cols), lambda i: (0, i)),
            pl.BlockSpec((pair_rows, cols), lambda i: (0, i)),
        ],
        out_specs=[
            pl.BlockSpec((rows, cols), lambda i: (0, i)),
            pl.BlockSpec((rows, cols), lambda i: (0, i)),
            pl.BlockSpec((SUMMED, 128), lambda i: (0, 0)),
            pl.BlockSpec((count, rows), lambda i: (0, 0)),
            pl.BlockSpec((count, rows), lambda i: (0, 0)),
        ],
        out_shape=[
            jax.ShapeDtypeStruct((rows, width), jnp.bfloat16),
            jax.ShapeDtypeStruct((rows, width), jnp.bfloat16),
            jax.ShapeDtypeStruct((SUMMED, 128), jnp.float32),
            jax.ShapeDtypeStruct((count, rows), jnp.float32),
            jax.ShapeDtypeStruct((count, rows), jnp.bfloat16),
        ],
        scratch_shapes=[
            pltpu.VMEM((count, pair_rows), jnp.float32),
            pltpu.VMEM((1, cols), jnp.float32),
        ],
        compiler_params=pltpu.CompilerParams(vmem_limit_bytes=VMEM_BYTES),
        cost_estimate=pl.CostEstimate(
            flops=4 * pair_rows * count * width,
            bytes_accessed=2 * (count * width + 3 * pair_rows * width + 4 * count * rows),
            transcendentals=0,
        ),
        name="products",
    )(heads_t, tokens, weight)


def finish_kernel(
    multiplier, spot_ref, weight_ref, partner_ref, here_ref, there_ref,
    partner_here_ref, partner_there_ref, part_ref, from_pair_ref, squares_ref, new_ref, heads_ref,
):
    entries = jnp.float32(4096 * 5120)
    here = pl.program_id(0) == 0
    own = spot_ref[1]

    def scale(index):
        part = squares_ref[pl.ds(index * (SUMMED // 2), SUMMED // 2), :]
        total = jnp.sum(part, axis=0, keepdims=True) * (multiplier * multiplier)
        factor = jnp.minimum(1.0, jnp.sqrt(entries) / jnp.sqrt(total))
        return (step_rate * multiplier * factor)[:, :1]

    def stepped(block_ref, amount, first_ref, second_ref):
        grad = jnp.where(here, first_ref[...], second_ref[...]).astype(jnp.float32)
        new = block_ref[...].astype(jnp.float32) - amount * grad
        return new.astype(jnp.bfloat16).astype(jnp.float32)

    mine = stepped(weight_ref, scale(own), here_ref, there_ref)
    theirs = stepped(partner_ref, scale(1 - own), partner_here_ref, partner_there_ref)
    new_ref[...] = ((mine + theirs) * 0.5).astype(new_ref.dtype)
    heads_ref[...] = (
        multiplier * (part_ref[...] + from_pair_ref[...].astype(jnp.float32))
    ).astype(heads_ref.dtype)


def finish(multiplier, spot, squares, weight, partner, grads, partner_grads, part, from_pair, blocks=1):
    rows, width = weight.shape
    half = width // 2
    cols = half // blocks
    count = part.shape[0]
    piece = count // (2 * blocks)

    def whole(h, i, spot_ref):
        return (0, jnp.where(h == 0, spot_ref[0], 1 - spot_ref[0]) * blocks + i)

    first = lambda h, i, *_: (0, jnp.where(h == 0, i, blocks - 1))
    second = lambda h, i, *_: (0, jnp.where(h == 0, 0, i))
    down = lambda h, i, *_: (h * blocks + i, 0)
    wide = pl.BlockSpec((rows, cols), whole)
    return pl.pallas_call(
        partial(finish_kernel, multiplier),
        grid_spec=pltpu.PrefetchScalarGridSpec(
            num_scalar_prefetch=1,
            grid=(2, blocks),
            in_specs=[
                wide,
                wide,
                pl.BlockSpec((rows, cols), first),
                pl.BlockSpec((rows, cols), second),
                pl.BlockSpec((rows, cols), first),
                pl.BlockSpec((rows, cols), second),
                pl.BlockSpec((piece, rows), down),
                pl.BlockSpec((piece, rows), down),
                pl.BlockSpec((SUMMED, 128), lambda h, i, *_: (0, 0)),
            ],
            out_specs=[wide, pl.BlockSpec((piece, rows), down)],
        ),
        out_shape=[
            jax.ShapeDtypeStruct((rows, width), jnp.bfloat16),
            jax.ShapeDtypeStruct((count, rows), jnp.bfloat16),
        ],
        compiler_params=pltpu.CompilerParams(vmem_limit_bytes=VMEM_BYTES),
        cost_estimate=pl.CostEstimate(
            flops=8 * rows * width, bytes_accessed=10 * rows * width + 8 * count * rows,
            transcendentals=0,
        ),
        name="finish",
    )(spot, weight, partner, *grads, *partner_grads, part, from_pair, squares)


def one_step(level, head_outputs, out_weight, cotangent):
    heads = head_outputs[0]
    weight = out_weight[0]
    tokens = cotangent[0]
    rows, width = weight.shape
    half = width // 2
    partner_axis = PARTNER_AXES[level]
    x = lax.axis_index("x")
    own = lax.axis_index(partner_axis)

    def mine(block):
        return lax.dynamic_slice_in_dim(block, x * half, half, axis=1)

    def other(block):
        return lax.dynamic_slice_in_dim(block, (1 - x) * half, half, axis=1)

    def swap(block):
        return lax.ppermute(block, "x", PAIR)

    def to_partner(block):
        return lax.ppermute(block, partner_axis, PAIR)

    def across(block):
        return lax.ppermute(block, (partner_axis, "x"), [(0, 3), (1, 2), (2, 1), (3, 0)])

    kept = mine(tokens)
    got = swap(other(tokens))
    pair_tokens = jnp.where(
        x == 0, jnp.concatenate([kept, got], 0), jnp.concatenate([got, kept], 0)
    )
    gathered = lax.all_gather(pair_tokens, Z, axis=0, tiled=True)

    heads_t = jnp.concatenate([heads, swap(heads)], 1).T
    weight_pair = jnp.concatenate([mine(weight), swap(other(weight))], 0)
    partner_weight = to_partner(weight)

    gathered, partner_weight, weight_pair = lax.optimization_barrier(
        (gathered, partner_weight, weight_pair)
    )
    here, there, squares, part_here, part_there = products(heads_t, gathered, weight_pair)
    partner_there = across(there)
    there = swap(there)
    partner_here = to_partner(here)
    from_pair = swap(part_there)
    squares = lax.all_to_all(squares, (partner_axis, *Z, "x"), 0, 0, tiled=True)

    return (
        own, squares, partner_weight, (here, there), (partner_here, partner_there), part_here,
        from_pair,
    )


def per_device(step, head_outputs, out_weight, cotangent):
    branches = [partial(one_step, level) for level in range(len(PARTNER_AXES))]
    own, squares, partner_weight, grads, partner_grads, part_here, from_pair = lax.switch(
        step[0] % len(PARTNER_AXES), branches, head_outputs, out_weight, cotangent
    )
    weight = out_weight[0]
    new_weight, head_grads = finish(
        float(weight.shape[0] * 32) ** (-0.5),
        jnp.stack([lax.axis_index("x"), own]).astype(jnp.int32),
        squares,
        weight,
        partner_weight,
        grads,
        partner_grads,
        part_here,
        from_pair,
    )
    return (new_weight[None], head_grads[None])


def solution(mesh):
    mesh = Mesh(
        mesh.devices.reshape(2, 2, 2, 2, 4, 4, 2), ("x_hi", "yh", "yl", "core", "zh", "zl", "x")
    )
    replica = ("x_hi", "yh", "yl", "core")
    tensor = ("zh", "zl", "x")
    return jax.shard_map(
        per_device,
        mesh=mesh,
        in_specs=(
            P(),
            P(replica, None, tensor),
            P(replica, tensor, None),
            P(replica, tensor, None),
        ),
        out_specs=(P(replica, tensor, None), P(replica, None, tensor)),
        check_vma=False,
    )
```

```python
from functools import partial

import jax
import jax.numpy as jnp
from jax import lax
from jax.experimental import pallas as pl
from jax.experimental.pallas import tpu as pltpu
from jax.sharding import Mesh, PartitionSpec as P

step_rate = 0.5
PAIR = [(0, 1), (1, 0)]
Z = ("zh", "zl")
PARTNER_AXES = ("core", "yl", "yh")
VMEM_BYTES = 48 * 1024 * 1024
SUMMED = 64


def gradient_kernel(heads_ref, tokens_ref, here_ref, there_ref, squares_ref, sums):
    rows = here_ref.shape[0]
    step, last = pl.program_id(0), pl.num_programs(0) - 1
    grad = jnp.dot(heads_ref[...], tokens_ref[...], preferred_element_type=jnp.float32)
    here_ref[...] = grad[:rows].astype(here_ref.dtype)
    there_ref[...] = grad[rows:].astype(there_ref.dtype)
    column_sums = jnp.sum(grad * grad, axis=0, keepdims=True)

    @pl.when(step == 0)
    def _():
        sums[...] = column_sums

    @pl.when(step > 0)
    def _():
        sums[...] += column_sums

    @pl.when(step == last)
    def _():
        squares_ref[...] = jnp.full(squares_ref.shape, jnp.sum(sums[...]), jnp.float32)


def gradient(heads_t, tokens, blocks=2):
    pair_rows, count = heads_t.shape
    rows, width = pair_rows // 2, tokens.shape[1]
    cols = width // blocks
    return pl.pallas_call(
        gradient_kernel,
        grid=(blocks,),
        in_specs=[
            pl.BlockSpec((pair_rows, count), lambda i: (0, 0)),
            pl.BlockSpec((count, cols), lambda i: (0, i)),
        ],
        out_specs=[
            pl.BlockSpec((rows, cols), lambda i: (0, i)),
            pl.BlockSpec((rows, cols), lambda i: (0, i)),
            pl.BlockSpec((SUMMED, 128), lambda i: (0, 0)),
        ],
        out_shape=[
            jax.ShapeDtypeStruct((rows, width), jnp.bfloat16),
            jax.ShapeDtypeStruct((rows, width), jnp.bfloat16),
            jax.ShapeDtypeStruct((SUMMED, 128), jnp.float32),
        ],
        scratch_shapes=[pltpu.VMEM((1, cols), jnp.float32)],
        compiler_params=pltpu.CompilerParams(vmem_limit_bytes=VMEM_BYTES),
        cost_estimate=pl.CostEstimate(
            flops=2 * pair_rows * count * width,
            bytes_accessed=2 * (count * width + pair_rows * width + pair_rows * count),
            transcendentals=0,
        ),
        name="gradient",
    )(heads_t, tokens)


def head_parts_kernel(tokens_ref, weight_ref, here_ref, there_ref):
    rows = here_ref.shape[1]
    part = lax.dot_general(
        tokens_ref[...], weight_ref[...], (((1,), (1,)), ((), ())),
        preferred_element_type=jnp.float32,
    )
    here_ref[...] = part[:, :rows]
    there_ref[...] = part[:, rows:].astype(there_ref.dtype)


def head_parts(tokens, weight, blocks=2):
    count, width = tokens.shape
    pair_rows = weight.shape[0]
    rows, piece = pair_rows // 2, count // blocks
    return pl.pallas_call(
        head_parts_kernel,
        grid=(blocks,),
        in_specs=[
            pl.BlockSpec((piece, width), lambda i: (i, 0)),
            pl.BlockSpec((pair_rows, width), lambda i: (0, 0)),
        ],
        out_specs=[pl.BlockSpec((piece, rows), lambda i: (i, 0))] * 2,
        out_shape=[
            jax.ShapeDtypeStruct((count, rows), jnp.float32),
            jax.ShapeDtypeStruct((count, rows), jnp.bfloat16),
        ],
        compiler_params=pltpu.CompilerParams(vmem_limit_bytes=VMEM_BYTES),
        cost_estimate=pl.CostEstimate(
            flops=2 * pair_rows * count * width,
            bytes_accessed=2 * (count * width + pair_rows * width + 3 * rows * count),
            transcendentals=0,
        ),
        name="head_parts",
    )(tokens, weight)


def finish_kernel(
    multiplier, spot_ref, weight_ref, partner_ref, here_ref, there_ref,
    partner_here_ref, partner_there_ref, part_ref, from_pair_ref, squares_ref, new_ref, heads_ref,
):
    entries = jnp.float32(4096 * 5120)
    own = spot_ref[1]

    def scale(index):
        part = squares_ref[pl.ds(index * (SUMMED // 2), SUMMED // 2), :]
        total = jnp.sum(part, axis=0, keepdims=True) * (multiplier * multiplier)
        factor = jnp.minimum(1.0, jnp.sqrt(entries) / jnp.sqrt(total))
        return (step_rate * multiplier * factor)[:, :1]

    def stepped(block_ref, amount, grad_ref):
        new = block_ref[...].astype(jnp.float32) - amount * grad_ref[...].astype(jnp.float32)
        return new.astype(jnp.bfloat16)

    def average(grad_ref, partner_grad_ref):
        mine = stepped(weight_ref, scale(own), grad_ref)
        theirs = stepped(partner_ref, scale(1 - own), partner_grad_ref)
        new_ref[...] = (mine + theirs) * jnp.bfloat16(0.5)

    @pl.when(pl.program_id(0) == 0)
    def _():
        average(here_ref, partner_here_ref)

    @pl.when(pl.program_id(0) == 1)
    def _():
        average(there_ref, partner_there_ref)

    heads_ref[...] = (
        multiplier * (part_ref[...] + from_pair_ref[...].astype(jnp.float32))
    ).astype(heads_ref.dtype)


def finish(multiplier, spot, squares, weight, partner, grads, partner_grads, part, from_pair, blocks=1):
    rows, width = weight.shape
    half = width // 2
    cols = half // blocks
    count = part.shape[0]
    piece = count // (2 * blocks)

    def whole(h, i, spot_ref):
        return (0, jnp.where(h == 0, spot_ref[0], 1 - spot_ref[0]) * blocks + i)

    first = lambda h, i, *_: (0, jnp.where(h == 0, i, blocks - 1))
    second = lambda h, i, *_: (0, jnp.where(h == 0, 0, i))
    down = lambda h, i, *_: (h * blocks + i, 0)
    wide = pl.BlockSpec((rows, cols), whole)
    return pl.pallas_call(
        partial(finish_kernel, multiplier),
        grid_spec=pltpu.PrefetchScalarGridSpec(
            num_scalar_prefetch=1,
            grid=(2, blocks),
            in_specs=[
                wide,
                wide,
                pl.BlockSpec((rows, cols), first),
                pl.BlockSpec((rows, cols), second),
                pl.BlockSpec((rows, cols), first),
                pl.BlockSpec((rows, cols), second),
                pl.BlockSpec((piece, rows), down),
                pl.BlockSpec((piece, rows), down),
                pl.BlockSpec((SUMMED, 128), lambda h, i, *_: (0, 0)),
            ],
            out_specs=[wide, pl.BlockSpec((piece, rows), down)],
        ),
        out_shape=[
            jax.ShapeDtypeStruct((rows, width), jnp.bfloat16),
            jax.ShapeDtypeStruct((count, rows), jnp.bfloat16),
        ],
        compiler_params=pltpu.CompilerParams(vmem_limit_bytes=VMEM_BYTES),
        cost_estimate=pl.CostEstimate(
            flops=8 * rows * width, bytes_accessed=10 * rows * width + 8 * count * rows,
            transcendentals=0,
        ),
        name="finish",
    )(spot, weight, partner, *grads, *partner_grads, part, from_pair, squares)


def one_step(level, head_outputs, out_weight, cotangent):
    heads = head_outputs[0]
    weight = out_weight[0]
    tokens = cotangent[0]
    rows, width = weight.shape
    half = width // 2
    partner_axis = PARTNER_AXES[level]
    x = lax.axis_index("x")
    own = lax.axis_index(partner_axis)

    def mine(block):
        return lax.dynamic_slice_in_dim(block, x * half, half, axis=1)

    def other(block):
        return lax.dynamic_slice_in_dim(block, (1 - x) * half, half, axis=1)

    def swap(block):
        return lax.ppermute(block, "x", PAIR)

    def to_partner(block):
        return lax.ppermute(block, partner_axis, PAIR)

    def across(block):
        return lax.ppermute(block, (partner_axis, "x"), [(0, 3), (1, 2), (2, 1), (3, 0)])

    kept = mine(tokens)
    got = swap(other(tokens))
    pair_tokens = jnp.where(
        x == 0, jnp.concatenate([kept, got], 0), jnp.concatenate([got, kept], 0)
    )
    gathered = lax.all_gather(pair_tokens, Z, axis=0, tiled=True)

    heads_t = jnp.concatenate([heads, swap(heads)], 1).T
    weight_pair = jnp.concatenate([mine(weight), swap(other(weight))], 0)
    partner_weight = to_partner(weight)

    gathered, partner_weight, weight_pair = lax.optimization_barrier(
        (gathered, partner_weight, weight_pair)
    )
    here, there, squares = gradient(heads_t, gathered)
    partner_there = across(there)
    there = swap(there)
    partner_here = to_partner(here)
    part_here, part_there = head_parts(gathered, weight_pair)
    from_pair = swap(part_there)
    squares, part_there = lax.optimization_barrier((squares, part_there))
    squares = lax.all_to_all(squares, (partner_axis, *Z, "x"), 0, 0, tiled=True)

    return (
        own, squares, partner_weight, (here, there), (partner_here, partner_there), part_here,
        from_pair,
    )


def per_device(step, head_outputs, out_weight, cotangent):
    branches = [partial(one_step, level) for level in range(len(PARTNER_AXES))]
    own, squares, partner_weight, grads, partner_grads, part_here, from_pair = lax.switch(
        step[0] % len(PARTNER_AXES), branches, head_outputs, out_weight, cotangent
    )
    weight = out_weight[0]
    new_weight, head_grads = finish(
        float(weight.shape[0] * 32) ** (-0.5),
        jnp.stack([lax.axis_index("x"), own]).astype(jnp.int32),
        squares,
        weight,
        partner_weight,
        grads,
        partner_grads,
        part_here,
        from_pair,
    )
    return (new_weight[None], head_grads[None])


def solution(mesh):
    mesh = Mesh(
        mesh.devices.reshape(2, 2, 2, 2, 4, 4, 2), ("x_hi", "yh", "yl", "core", "zh", "zl", "x")
    )
    replica = ("x_hi", "yh", "yl", "core")
    tensor = ("zh", "zl", "x")
    return jax.shard_map(
        per_device,
        mesh=mesh,
        in_specs=(
            P(),
            P(replica, None, tensor),
            P(replica, tensor, None),
            P(replica, tensor, None),
        ),
        out_specs=(P(replica, tensor, None), P(replica, None, tensor)),
        check_vma=False,
    )
```

```python
from functools import partial

import jax
import jax.numpy as jnp
from jax import lax
from jax.experimental import pallas as pl
from jax.experimental.pallas import tpu as pltpu
from jax.sharding import Mesh, PartitionSpec as P

step_rate = 0.5
PAIR = [(0, 1), (1, 0)]
Z = ("zh", "zl")
PARTNER_AXES = ("core", "yl", "yh")
VMEM_BYTES = 48 * 1024 * 1024
SUMMED = 64


def gradient_kernel(heads_ref, tokens_ref, here_ref, there_ref, squares_ref, sums):
    rows = here_ref.shape[0]
    step, last = pl.program_id(0), pl.num_programs(0) - 1
    grad = jnp.dot(heads_ref[...], tokens_ref[...], preferred_element_type=jnp.float32)
    here_ref[...] = grad[:rows].astype(here_ref.dtype)
    there_ref[...] = grad[rows:].astype(there_ref.dtype)
    column_sums = jnp.sum(grad * grad, axis=0, keepdims=True)

    @pl.when(step == 0)
    def _():
        sums[...] = column_sums

    @pl.when(step > 0)
    def _():
        sums[...] += column_sums

    @pl.when(step == last)
    def _():
        squares_ref[...] = jnp.full(squares_ref.shape, jnp.sum(sums[...]), jnp.float32)


def gradient(heads_t, tokens, blocks=2):
    pair_rows, count = heads_t.shape
    rows, width = pair_rows // 2, tokens.shape[1]
    cols = width // blocks
    return pl.pallas_call(
        gradient_kernel,
        grid=(blocks,),
        in_specs=[
            pl.BlockSpec((pair_rows, count), lambda i: (0, 0)),
            pl.BlockSpec((count, cols), lambda i: (0, i)),
        ],
        out_specs=[
            pl.BlockSpec((rows, cols), lambda i: (0, i)),
            pl.BlockSpec((rows, cols), lambda i: (0, i)),
            pl.BlockSpec((SUMMED, 128), lambda i: (0, 0)),
        ],
        out_shape=[
            jax.ShapeDtypeStruct((rows, width), jnp.bfloat16),
            jax.ShapeDtypeStruct((rows, width), jnp.bfloat16),
            jax.ShapeDtypeStruct((SUMMED, 128), jnp.float32),
        ],
        scratch_shapes=[pltpu.VMEM((1, cols), jnp.float32)],
        compiler_params=pltpu.CompilerParams(vmem_limit_bytes=VMEM_BYTES),
        cost_estimate=pl.CostEstimate(
            flops=2 * pair_rows * count * width,
            bytes_accessed=2 * (count * width + pair_rows * width + pair_rows * count),
            transcendentals=0,
        ),
        name="gradient",
    )(heads_t, tokens)


def head_parts_kernel(tokens_ref, weight_ref, here_ref, there_ref):
    rows = here_ref.shape[1]
    part = lax.dot_general(
        tokens_ref[...], weight_ref[...], (((1,), (1,)), ((), ())),
        preferred_element_type=jnp.float32,
    )
    here_ref[...] = part[:, :rows]
    there_ref[...] = part[:, rows:].astype(there_ref.dtype)


def head_parts(tokens, weight, blocks=2):
    count, width = tokens.shape
    pair_rows = weight.shape[0]
    rows, piece = pair_rows // 2, count // blocks
    return pl.pallas_call(
        head_parts_kernel,
        grid=(blocks,),
        in_specs=[
            pl.BlockSpec((piece, width), lambda i: (i, 0)),
            pl.BlockSpec((pair_rows, width), lambda i: (0, 0)),
        ],
        out_specs=[pl.BlockSpec((piece, rows), lambda i: (i, 0))] * 2,
        out_shape=[
            jax.ShapeDtypeStruct((count, rows), jnp.float32),
            jax.ShapeDtypeStruct((count, rows), jnp.bfloat16),
        ],
        compiler_params=pltpu.CompilerParams(vmem_limit_bytes=VMEM_BYTES),
        cost_estimate=pl.CostEstimate(
            flops=2 * pair_rows * count * width,
            bytes_accessed=2 * (count * width + pair_rows * width + 3 * rows * count),
            transcendentals=0,
        ),
        name="head_parts",
    )(tokens, weight)


def average_kernel(
    multiplier, spot_ref, weight_ref, partner_ref, here_ref, there_ref, partner_here_ref,
    partner_there_ref, squares_ref, new_ref,
):
    entries = jnp.float32(4096 * 5120)
    own = spot_ref[1]

    def scale(index):
        part = squares_ref[pl.ds(index * (SUMMED // 2), SUMMED // 2), :]
        total = jnp.sum(part, axis=0, keepdims=True) * (multiplier * multiplier)
        factor = jnp.minimum(1.0, jnp.sqrt(entries) / jnp.sqrt(total))
        return (step_rate * multiplier * factor)[:, :1]

    def stepped(block_ref, amount, grad_ref):
        new = block_ref[...].astype(jnp.float32) - amount * grad_ref[...].astype(jnp.float32)
        return new.astype(jnp.bfloat16)

    def average(grad_ref, partner_grad_ref):
        mine = stepped(weight_ref, scale(own), grad_ref)
        theirs = stepped(partner_ref, scale(1 - own), partner_grad_ref)
        new_ref[0] = (mine + theirs) * jnp.bfloat16(0.5)

    @pl.when(pl.program_id(0) == 0)
    def _():
        average(here_ref, partner_here_ref)

    @pl.when(pl.program_id(0) == 1)
    def _():
        average(there_ref, partner_there_ref)


def averaged(multiplier, spot, squares, weight, partner, grads, partner_grads):
    rows, width = weight.shape
    half = width // 2

    def side(h, spot_ref):
        return jnp.where(h == 0, spot_ref[0], 1 - spot_ref[0])

    wide = pl.BlockSpec((rows, half), lambda h, spot_ref: (0, side(h, spot_ref)))
    whole = pl.BlockSpec((rows, half), lambda h, spot_ref: (0, 0))
    return pl.pallas_call(
        partial(average_kernel, multiplier),
        grid_spec=pltpu.PrefetchScalarGridSpec(
            num_scalar_prefetch=1,
            grid=(2,),
            in_specs=[wide, wide]
            + [whole] * 4
            + [pl.BlockSpec((SUMMED, 128), lambda h, spot_ref: (0, 0))],
            out_specs=pl.BlockSpec((1, rows, half), lambda h, spot_ref: (0, 0, side(h, spot_ref))),
        ),
        out_shape=jax.ShapeDtypeStruct((1, rows, width), jnp.bfloat16),
        compiler_params=pltpu.CompilerParams(vmem_limit_bytes=VMEM_BYTES),
        cost_estimate=pl.CostEstimate(
            flops=8 * rows * width, bytes_accessed=10 * rows * width, transcendentals=0
        ),
        name="averaged",
    )(spot, weight, partner, *grads, *partner_grads, squares)


def one_step(level, head_outputs, out_weight, cotangent):
    heads = head_outputs[0]
    weight = out_weight[0]
    tokens = cotangent[0]
    rows, width = weight.shape
    half = width // 2
    partner_axis = PARTNER_AXES[level]
    x = lax.axis_index("x")
    own = lax.axis_index(partner_axis)

    def mine(block):
        return lax.dynamic_slice_in_dim(block, x * half, half, axis=1)

    def other(block):
        return lax.dynamic_slice_in_dim(block, (1 - x) * half, half, axis=1)

    def swap(block):
        return lax.ppermute(block, "x", PAIR)

    def to_partner(block):
        return lax.ppermute(block, partner_axis, PAIR)

    def across(block):
        return lax.ppermute(block, (partner_axis, "x"), [(0, 3), (1, 2), (2, 1), (3, 0)])

    kept = mine(tokens)
    got = swap(other(tokens))
    pair_tokens = jnp.where(
        x == 0, jnp.concatenate([kept, got], 0), jnp.concatenate([got, kept], 0)
    )
    gathered = lax.all_gather(pair_tokens, Z, axis=0, tiled=True)

    heads_t = jnp.concatenate([heads, swap(heads)], 1).T
    weight_pair = jnp.concatenate([mine(weight), swap(other(weight))], 0)
    partner_weight = to_partner(weight)

    gathered, partner_weight, weight_pair, heads_t = lax.optimization_barrier(
        (gathered, partner_weight, weight_pair, heads_t)
    )
    part_here, part_there = head_parts(gathered, weight_pair)
    from_pair = swap(part_there)
    heads_t, part_there = lax.optimization_barrier((heads_t, part_there))
    here, there, squares = gradient(heads_t, gathered)
    partner_there = across(there)
    there = swap(there)
    partner_here = to_partner(here)
    squares = lax.all_to_all(squares, (partner_axis, *Z, "x"), 0, 0, tiled=True)

    multiplier = float(rows * 32) ** (-0.5)
    new_weight = averaged(
        multiplier,
        jnp.stack([x, own]).astype(jnp.int32),
        squares,
        weight,
        partner_weight,
        (here, there),
        (partner_here, partner_there),
    )
    head_grads = (multiplier * (part_here + from_pair.astype(jnp.float32))).astype(jnp.bfloat16)
    return new_weight, head_grads[None]


def per_device(step, head_outputs, out_weight, cotangent):
    branches = [partial(one_step, level) for level in range(len(PARTNER_AXES))]
    return lax.switch(
        step[0] % len(PARTNER_AXES), branches, head_outputs, out_weight, cotangent
    )


def solution(mesh):
    mesh = Mesh(
        mesh.devices.reshape(2, 2, 2, 2, 4, 4, 2), ("x_hi", "yh", "yl", "core", "zh", "zl", "x")
    )
    replica = ("x_hi", "yh", "yl", "core")
    tensor = ("zh", "zl", "x")
    return jax.shard_map(
        per_device,
        mesh=mesh,
        in_specs=(
            P(),
            P(replica, None, tensor),
            P(replica, tensor, None),
            P(replica, tensor, None),
        ),
        out_specs=(P(replica, tensor, None), P(replica, None, tensor)),
        check_vma=False,
    )
```

```python
from functools import partial

import jax
import jax.numpy as jnp
from jax import lax
from jax.experimental import pallas as pl
from jax.experimental.pallas import tpu as pltpu
from jax.sharding import Mesh, PartitionSpec as P

step_rate = 0.5
PAIR = [(0, 1), (1, 0)]
Z = ("zh", "zl")
PARTNER_AXES = ("core", "yl", "yh")
VMEM_BYTES = 48 * 1024 * 1024
SUMMED = 64


def gradient_kernel(heads_ref, tokens_ref, here_ref, there_ref, squares_ref, sums):
    rows = here_ref.shape[0]
    step, last = pl.program_id(0), pl.num_programs(0) - 1
    grad = jnp.dot(heads_ref[...], tokens_ref[...], preferred_element_type=jnp.float32)
    here_ref[...] = grad[:rows].astype(here_ref.dtype)
    there_ref[...] = grad[rows:].astype(there_ref.dtype)
    column_sums = jnp.sum(grad * grad, axis=0, keepdims=True)

    @pl.when(step == 0)
    def _():
        sums[...] = column_sums

    @pl.when(step > 0)
    def _():
        sums[...] += column_sums

    @pl.when(step == last)
    def _():
        squares_ref[...] = jnp.full(squares_ref.shape, jnp.sum(sums[...]), jnp.float32)


def gradient(heads_t, tokens, blocks=2):
    pair_rows, count = heads_t.shape
    rows, width = pair_rows // 2, tokens.shape[1]
    cols = width // blocks
    return pl.pallas_call(
        gradient_kernel,
        grid=(blocks,),
        in_specs=[
            pl.BlockSpec((pair_rows, count), lambda i: (0, 0)),
            pl.BlockSpec((count, cols), lambda i: (0, i)),
        ],
        out_specs=[
            pl.BlockSpec((rows, cols), lambda i: (0, i)),
            pl.BlockSpec((rows, cols), lambda i: (0, i)),
            pl.BlockSpec((SUMMED, 128), lambda i: (0, 0)),
        ],
        out_shape=[
            jax.ShapeDtypeStruct((rows, width), jnp.bfloat16),
            jax.ShapeDtypeStruct((rows, width), jnp.bfloat16),
            jax.ShapeDtypeStruct((SUMMED, 128), jnp.float32),
        ],
        scratch_shapes=[pltpu.VMEM((1, cols), jnp.float32)],
        compiler_params=pltpu.CompilerParams(vmem_limit_bytes=VMEM_BYTES),
        cost_estimate=pl.CostEstimate(
            flops=2 * pair_rows * count * width,
            bytes_accessed=2 * (count * width + pair_rows * width + pair_rows * count),
            transcendentals=0,
        ),
        name="gradient",
    )(heads_t, tokens)


def head_parts_kernel(tokens_ref, weight_ref, here_ref, there_ref):
    rows = here_ref.shape[1]
    part = lax.dot_general(
        tokens_ref[...], weight_ref[...], (((1,), (1,)), ((), ())),
        preferred_element_type=jnp.float32,
    )
    here_ref[...] = part[:, :rows]
    there_ref[...] = part[:, rows:].astype(there_ref.dtype)


def head_parts(tokens, weight, blocks=2):
    count, width = tokens.shape
    pair_rows = weight.shape[0]
    rows, piece = pair_rows // 2, count // blocks
    return pl.pallas_call(
        head_parts_kernel,
        grid=(blocks,),
        in_specs=[
            pl.BlockSpec((piece, width), lambda i: (i, 0)),
            pl.BlockSpec((pair_rows, width), lambda i: (0, 0)),
        ],
        out_specs=[pl.BlockSpec((piece, rows), lambda i: (i, 0))] * 2,
        out_shape=[
            jax.ShapeDtypeStruct((count, rows), jnp.float32),
            jax.ShapeDtypeStruct((count, rows), jnp.bfloat16),
        ],
        compiler_params=pltpu.CompilerParams(vmem_limit_bytes=VMEM_BYTES),
        cost_estimate=pl.CostEstimate(
            flops=2 * pair_rows * count * width,
            bytes_accessed=2 * (count * width + pair_rows * width + 3 * rows * count),
            transcendentals=0,
        ),
        name="head_parts",
    )(tokens, weight)


def average_kernel(
    multiplier, spot_ref, weight_ref, partner_ref, here_ref, there_ref, partner_here_ref,
    partner_there_ref, squares_ref, new_ref,
):
    entries = jnp.float32(4096 * 5120)
    own = spot_ref[1]

    def scale(index):
        part = squares_ref[pl.ds(index * (SUMMED // 2), SUMMED // 2), :]
        total = jnp.sum(part, axis=0, keepdims=True) * (multiplier * multiplier)
        factor = jnp.minimum(1.0, jnp.sqrt(entries) / jnp.sqrt(total))
        return (step_rate * multiplier * factor)[:, :1]

    amount, partner_amount = scale(own), scale(1 - own)
    half = here_ref.shape[1]

    def stepped(block, amount, grad_ref):
        new = block.astype(jnp.float32) - amount * grad_ref[...].astype(jnp.float32)
        return new.astype(jnp.bfloat16)

    def average(side, grad_ref, partner_grad_ref):
        columns = pl.ds(pl.multiple_of(side * half, 128), half)
        mine = stepped(weight_ref[:, columns], amount, grad_ref)
        theirs = stepped(partner_ref[:, columns], partner_amount, partner_grad_ref)
        new_ref[0, :, columns] = (mine + theirs) * jnp.bfloat16(0.5)

    average(spot_ref[0], here_ref, partner_here_ref)
    average(1 - spot_ref[0], there_ref, partner_there_ref)


def averaged(multiplier, spot, squares, weight, partner, grads, partner_grads):
    rows, width = weight.shape
    whole = pl.BlockSpec(memory_space=pltpu.VMEM)
    return pl.pallas_call(
        partial(average_kernel, multiplier),
        in_specs=[pl.BlockSpec(memory_space=pltpu.SMEM)] + [whole] * 7,
        out_specs=whole,
        out_shape=jax.ShapeDtypeStruct((1, rows, width), jnp.bfloat16),
        compiler_params=pltpu.CompilerParams(vmem_limit_bytes=VMEM_BYTES),
        cost_estimate=pl.CostEstimate(
            flops=8 * rows * width, bytes_accessed=10 * rows * width, transcendentals=0
        ),
        name="averaged",
    )(spot, weight, partner, *grads, *partner_grads, squares)


def one_step(level, head_outputs, out_weight, cotangent):
    heads = head_outputs[0]
    weight = out_weight[0]
    tokens = cotangent[0]
    rows, width = weight.shape
    half = width // 2
    partner_axis = PARTNER_AXES[level]
    x = lax.axis_index("x")
    own = lax.axis_index(partner_axis)

    def mine(block):
        return lax.dynamic_slice_in_dim(block, x * half, half, axis=1)

    def other(block):
        return lax.dynamic_slice_in_dim(block, (1 - x) * half, half, axis=1)

    def swap(block):
        return lax.ppermute(block, "x", PAIR)

    def to_partner(block):
        return lax.ppermute(block, partner_axis, PAIR)

    def across(block):
        return lax.ppermute(block, (partner_axis, "x"), [(0, 3), (1, 2), (2, 1), (3, 0)])

    kept = mine(tokens)
    got = swap(other(tokens))
    pair_tokens = jnp.where(
        x == 0, jnp.concatenate([kept, got], 0), jnp.concatenate([got, kept], 0)
    )
    gathered = lax.all_gather(pair_tokens, Z, axis=0, tiled=True)

    heads_t = jnp.concatenate([heads, swap(heads)], 1).T
    weight_pair = jnp.concatenate([mine(weight), swap(other(weight))], 0)
    partner_weight = to_partner(weight)

    gathered, partner_weight, weight_pair, heads_t = lax.optimization_barrier(
        (gathered, partner_weight, weight_pair, heads_t)
    )
    part_here, part_there = head_parts(gathered, weight_pair)
    from_pair = swap(part_there)
    heads_t, part_there = lax.optimization_barrier((heads_t, part_there))
    here, there, squares = gradient(heads_t, gathered)
    partner_there = across(there)
    there = swap(there)
    partner_here = to_partner(here)
    squares = lax.all_to_all(squares, (partner_axis, *Z, "x"), 0, 0, tiled=True)

    multiplier = float(rows * 32) ** (-0.5)
    new_weight = averaged(
        multiplier,
        jnp.stack([x, own]).astype(jnp.int32),
        squares,
        weight,
        partner_weight,
        (here, there),
        (partner_here, partner_there),
    )
    head_grads = (multiplier * (part_here + from_pair.astype(jnp.float32))).astype(jnp.bfloat16)
    return new_weight, head_grads[None]


def per_device(step, head_outputs, out_weight, cotangent):
    branches = [partial(one_step, level) for level in range(len(PARTNER_AXES))]
    return lax.switch(
        step[0] % len(PARTNER_AXES), branches, head_outputs, out_weight, cotangent
    )


def solution(mesh):
    mesh = Mesh(
        mesh.devices.reshape(2, 2, 2, 2, 4, 4, 2), ("x_hi", "yh", "yl", "core", "zh", "zl", "x")
    )
    replica = ("x_hi", "yh", "yl", "core")
    tensor = ("zh", "zl", "x")
    return jax.shard_map(
        per_device,
        mesh=mesh,
        in_specs=(
            P(),
            P(replica, None, tensor),
            P(replica, tensor, None),
            P(replica, tensor, None),
        ),
        out_specs=(P(replica, tensor, None), P(replica, None, tensor)),
        check_vma=False,
    )
```

```python
from functools import partial

import jax
import jax.numpy as jnp
from jax import lax
from jax.experimental import pallas as pl
from jax.experimental.pallas import tpu as pltpu
from jax.sharding import Mesh, PartitionSpec as P

step_rate = 0.5
PAIR = [(0, 1), (1, 0)]
Z = ("zh", "zl")
PARTNER_AXES = ("core", "yl", "yh")
VMEM_BYTES = 48 * 1024 * 1024
SUMMED = 64


def gradient_kernel(heads_ref, tokens_ref, here_ref, there_ref, squares_ref, sums):
    rows = here_ref.shape[0]
    step, last = pl.program_id(0), pl.num_programs(0) - 1
    grad = jnp.dot(heads_ref[...], tokens_ref[...], preferred_element_type=jnp.float32)
    here_ref[...] = grad[:rows].astype(here_ref.dtype)
    there_ref[...] = grad[rows:].astype(there_ref.dtype)
    column_sums = jnp.sum(grad * grad, axis=0, keepdims=True)

    @pl.when(step == 0)
    def _():
        sums[...] = column_sums

    @pl.when(step > 0)
    def _():
        sums[...] += column_sums

    @pl.when(step == last)
    def _():
        squares_ref[...] = jnp.full(squares_ref.shape, jnp.sum(sums[...]), jnp.float32)


def gradient(heads_t, tokens, blocks=2):
    pair_rows, count = heads_t.shape
    rows, width = pair_rows // 2, tokens.shape[1]
    cols = width // blocks
    return pl.pallas_call(
        gradient_kernel,
        grid=(blocks,),
        in_specs=[
            pl.BlockSpec((pair_rows, count), lambda i: (0, 0)),
            pl.BlockSpec((count, cols), lambda i: (0, i)),
        ],
        out_specs=[
            pl.BlockSpec((rows, cols), lambda i: (0, i)),
            pl.BlockSpec((rows, cols), lambda i: (0, i)),
            pl.BlockSpec((SUMMED, 128), lambda i: (0, 0)),
        ],
        out_shape=[
            jax.ShapeDtypeStruct((rows, width), jnp.bfloat16),
            jax.ShapeDtypeStruct((rows, width), jnp.bfloat16),
            jax.ShapeDtypeStruct((SUMMED, 128), jnp.float32),
        ],
        scratch_shapes=[pltpu.VMEM((1, cols), jnp.float32)],
        compiler_params=pltpu.CompilerParams(vmem_limit_bytes=VMEM_BYTES),
        cost_estimate=pl.CostEstimate(
            flops=2 * pair_rows * count * width,
            bytes_accessed=2 * (count * width + pair_rows * width + pair_rows * count),
            transcendentals=0,
        ),
        name="gradient",
    )(heads_t, tokens)


def head_parts_kernel(tokens_ref, weight_ref, here_ref, there_ref):
    rows = here_ref.shape[1]
    part = lax.dot_general(
        tokens_ref[...], weight_ref[...], (((1,), (1,)), ((), ())),
        preferred_element_type=jnp.float32,
    )
    here_ref[...] = part[:, :rows]
    there_ref[...] = part[:, rows:].astype(there_ref.dtype)


def head_parts(tokens, weight, blocks=2):
    count, width = tokens.shape
    pair_rows = weight.shape[0]
    rows, piece = pair_rows // 2, count // blocks
    return pl.pallas_call(
        head_parts_kernel,
        grid=(blocks,),
        in_specs=[
            pl.BlockSpec((piece, width), lambda i: (i, 0)),
            pl.BlockSpec((pair_rows, width), lambda i: (0, 0)),
        ],
        out_specs=[pl.BlockSpec((piece, rows), lambda i: (i, 0))] * 2,
        out_shape=[
            jax.ShapeDtypeStruct((count, rows), jnp.float32),
            jax.ShapeDtypeStruct((count, rows), jnp.bfloat16),
        ],
        compiler_params=pltpu.CompilerParams(vmem_limit_bytes=VMEM_BYTES),
        cost_estimate=pl.CostEstimate(
            flops=2 * pair_rows * count * width,
            bytes_accessed=2 * (count * width + pair_rows * width + 3 * rows * count),
            transcendentals=0,
        ),
        name="head_parts",
    )(tokens, weight)


def average_kernel(
    multiplier, spot_ref, weight_ref, partner_ref, here_ref, there_ref, partner_here_ref,
    partner_there_ref, squares_ref, new_ref,
):
    entries = jnp.float32(4096 * 5120)
    own = spot_ref[1]

    def scale(index):
        part = squares_ref[pl.ds(index * (SUMMED // 2), SUMMED // 2), :]
        total = jnp.sum(part, axis=0, keepdims=True) * (multiplier * multiplier)
        factor = jnp.minimum(1.0, jnp.sqrt(entries) / jnp.sqrt(total))
        return (step_rate * multiplier * factor)[:, :1]

    amount, partner_amount = scale(own), scale(1 - own)
    half = here_ref.shape[1]

    def stepped(block, amount, grad_ref):
        new = block.astype(jnp.float32) - amount * grad_ref[...].astype(jnp.float32)
        return new.astype(jnp.bfloat16)

    def average(side, grad_ref, partner_grad_ref):
        columns = pl.ds(pl.multiple_of(side * half, 128), half)
        mine = stepped(weight_ref[:, columns], amount, grad_ref)
        theirs = stepped(partner_ref[:, columns], partner_amount, partner_grad_ref)
        new_ref[0, :, columns] = (mine + theirs) * jnp.bfloat16(0.5)

    average(spot_ref[0], here_ref, partner_here_ref)
    average(1 - spot_ref[0], there_ref, partner_there_ref)


def averaged(multiplier, spot, squares, weight, partner, grads, partner_grads):
    rows, width = weight.shape
    whole = pl.BlockSpec(memory_space=pltpu.VMEM)
    return pl.pallas_call(
        partial(average_kernel, multiplier),
        in_specs=[pl.BlockSpec(memory_space=pltpu.SMEM)] + [whole] * 7,
        out_specs=whole,
        out_shape=jax.ShapeDtypeStruct((1, rows, width), jnp.bfloat16),
        compiler_params=pltpu.CompilerParams(vmem_limit_bytes=VMEM_BYTES),
        cost_estimate=pl.CostEstimate(
            flops=8 * rows * width, bytes_accessed=10 * rows * width, transcendentals=0
        ),
        name="averaged",
    )(spot, weight, partner, *grads, *partner_grads, squares)


def one_step(level, head_outputs, out_weight, cotangent):
    heads = head_outputs[0]
    weight = out_weight[0]
    tokens = cotangent[0]
    rows, width = weight.shape
    half = width // 2
    partner_axis = PARTNER_AXES[level]
    x = lax.axis_index("x")
    own = lax.axis_index(partner_axis)

    def mine(block):
        return lax.dynamic_slice_in_dim(block, x * half, half, axis=1)

    def other(block):
        return lax.dynamic_slice_in_dim(block, (1 - x) * half, half, axis=1)

    def swap(block):
        return lax.ppermute(block, "x", PAIR)

    def to_partner(block):
        return lax.ppermute(block, partner_axis, PAIR)

    def across(block):
        return lax.ppermute(block, (partner_axis, "x"), [(0, 3), (1, 2), (2, 1), (3, 0)])

    sent, tokens = lax.optimization_barrier((other(tokens), tokens))
    got = swap(sent)
    kept = mine(tokens)
    pair_tokens = jnp.where(
        x == 0, jnp.concatenate([kept, got], 0), jnp.concatenate([got, kept], 0)
    )
    gathered = lax.all_gather(pair_tokens, Z, axis=0, tiled=True)

    heads_t = jnp.concatenate([heads, swap(heads)], 1).T
    weight_pair = jnp.concatenate([mine(weight), swap(other(weight))], 0)
    partner_weight = to_partner(weight)

    gathered, partner_weight, weight_pair, heads_t = lax.optimization_barrier(
        (gathered, partner_weight, weight_pair, heads_t)
    )
    part_here, part_there = head_parts(gathered, weight_pair)
    from_pair = swap(part_there)
    heads_t, part_there = lax.optimization_barrier((heads_t, part_there))
    here, there, squares = gradient(heads_t, gathered)
    partner_there = across(there)
    there = swap(there)
    partner_here = to_partner(here)
    squares = lax.all_to_all(squares, (partner_axis, *Z, "x"), 0, 0, tiled=True)

    multiplier = float(rows * 32) ** (-0.5)
    new_weight = averaged(
        multiplier,
        jnp.stack([x, own]).astype(jnp.int32),
        squares,
        weight,
        partner_weight,
        (here, there),
        (partner_here, partner_there),
    )
    head_grads = (multiplier * (part_here + from_pair.astype(jnp.float32))).astype(jnp.bfloat16)
    return new_weight, head_grads[None]


def per_device(step, head_outputs, out_weight, cotangent):
    branches = [partial(one_step, level) for level in range(len(PARTNER_AXES))]
    return lax.switch(
        step[0] % len(PARTNER_AXES), branches, head_outputs, out_weight, cotangent
    )


def solution(mesh):
    mesh = Mesh(
        mesh.devices.reshape(2, 2, 2, 2, 4, 4, 2), ("x_hi", "yh", "yl", "core", "zh", "zl", "x")
    )
    replica = ("x_hi", "yh", "yl", "core")
    tensor = ("zh", "zl", "x")
    return jax.shard_map(
        per_device,
        mesh=mesh,
        in_specs=(
            P(),
            P(replica, None, tensor),
            P(replica, tensor, None),
            P(replica, tensor, None),
        ),
        out_specs=(P(replica, tensor, None), P(replica, None, tensor)),
        check_vma=False,
    )
```
